768 devices in a mesh: dp: 12 (over z), mp: 64 (over x, y, core).
Axes of the slice: x: 4, y: 8, z: 12, core: 2. Of those that a mesh axis runs over, the one named last changes fastest.
Arguments:
- query_states: bfloat16 [98304, 1024], P(('dp', 'mp')), may hold values from -6 to 6
- passage_states: bfloat16 [1105920, 1024], P(('dp', 'mp')), may hold values from -6 to 6
- proj_weight: bfloat16 [1024, 128], P('mp'), may hold values from -0.1875 to 0.1875
- negatives: int32 [3072, 32], P(('dp', 'mp')), may hold values from 0 to 6143, as said below
- ranks: int32 [3072, 32], P(('dp', 'mp')), may hold values from 0 to 31, each once within a row
Outputs:
- grad_queries: bfloat16 [98304, 1024], P(('dp', 'mp'))
- grad_weight: float32 [1024, 128], P('mp')
The draws below stay inside these ranges and needn't reach their ends.
Inputs may be any that keep to these rules, and one draw needn't show every extreme that they name: `negatives`: each row lists 32 different passages. Passage g is held by the device of index g // 8 in dp+mp order, and every listed passage of a query is held by a device whose mp index equals that of the query's own device. `ranks`: each row holds every rank of 0 to 31 once.
All inputs are finite; a program needn't handle non-finite values.
Results may differ from the reference program's by a relative error of at most 0.025.
Values may be sent and summed in bfloat16 or wider, within the bound.
No kernel may reach another device: no remote copies, remote signals or barrier semaphores. Data moves between devices by JAX's collectives and lax.ppermute only.
A program may use at most 128 MiB of HBM per device.

```python
import jax
import jax.numpy as jnp
from jax import lax

D = 1024
EMB = 128
QLEN = 32
PLEN = 180
NEG = 32
Q_DEV = 4
P_DEV = 8
NQUERIES = 3072
NPASSAGES = 6144
N_DP = 12
N_MP = 64


def draw_negatives(key, part):
    key = jax.random.fold_in(key, 11)
    embedding_dimension = N_DP * P_DEV
    favored_increment = jax.random.randint(jax.random.fold_in(key, 1), (N_MP, N_DP), 0, 3)
    noise_perturbation = jax.random.randint(jax.random.fold_in(key, 2), (NQUERIES, embedding_dimension), 0, 4)
    query = jnp.arange(NQUERIES, dtype=jnp.int32)
    feature_segment = query // Q_DEV % N_MP
    holder_processes = jnp.arange(embedding_dimension, dtype=jnp.int32) // P_DEV
    logit_addend = favored_increment[feature_segment][:, holder_processes]
    similarity_logits = (noise_perturbation + 2 * logit_addend) * embedding_dimension + jnp.arange(embedding_dimension, dtype=jnp.int32)[None, :]
    picked = lax.top_k(similarity_logits, NEG)[1].astype(jnp.int32)
    holder = picked // P_DEV * N_MP + feature_segment[:, None]
    return (holder * P_DEV + picked % P_DEV).astype(jnp.int32)


def levels(rng, shape, split, smallest, largest):
    def one(axis_at, shards_of):
        heights = jax.random.uniform(jax.random.fold_in(jax.random.fold_in(rng, 6), axis_at), (shards_of,), jnp.float32, smallest / len(split), largest / len(split))
        return jnp.repeat(jnp.exp(heights), shape[axis_at] // shards_of).reshape((-1,) + (1,) * (len(shape) - axis_at - 1))

    gain = one(*split[0])
    for cut in split[1:]:
        gain = gain * one(*cut)
    return gain


def centred(rng, extent, deviation, most, shards=(), kind=jnp.bfloat16):
    values = jax.random.normal(rng, extent, jnp.float32) * deviation
    if len(shards) > 0:
        values = levels(rng, extent, shards, -0.22, 0.18) * values
    return jnp.clip(values, min=-most, max=most).astype(kind)


def setup_inputs(seed: int = 0) -> dict:
    seeds = jax.random.split(jax.random.key(seed), 6)
    return {
        "query_states": centred(seeds[0], (NQUERIES * QLEN, D), 1.0, 6.0, ((0, 768),)),
        "passage_states": centred(seeds[1], (NPASSAGES * PLEN, D), 1.0, 6.0, ((0, 768),)),
        "proj_weight": centred(seeds[2], (D, EMB), D ** -0.5, 0.1875, ((0, 64),)),
        "negatives": draw_negatives(jax.random.fold_in(seeds[5], 71), 0),
        "ranks": jax.vmap(lambda own: jax.random.permutation(own, NEG))(jax.random.split(seeds[4], NQUERIES)).reshape((NQUERIES, NEG)).astype(jnp.int32),
    }


TAU = 0.1
RANK_TEMP = 8.0
EPS = 1e-06

def normalize(values):
    scale = lax.rsqrt(lax.optimization_barrier(jnp.sum(values * values, axis=-1, keepdims=True)) + EPS)
    return (values * scale, scale)

def token_weights(query_rows, passage_block):
    dots = jnp.dot(query_rows, passage_block.T, preferred_element_type=jnp.float32)
    expo = jnp.exp(dots / TAU)
    return (expo, lax.optimization_barrier(jnp.sum(expo, axis=1)))

def column_grads(feature_segment, query_states, passage_states, weight, negatives, ranks):
    q_rows = Q_DEV * QLEN
    p_rows = P_DEV * PLEN
    hq = lax.dynamic_index_in_dim(query_states.reshape(N_DP, N_MP, q_rows, D), feature_segment, 1, False).reshape(N_DP * q_rows, D)
    hp = lax.dynamic_index_in_dim(passage_states.reshape(N_DP, N_MP, p_rows, D), feature_segment, 1, False).reshape(N_DP * p_rows, D)
    neg_col = lax.dynamic_index_in_dim(negatives.reshape(N_DP, N_MP, Q_DEV, NEG), feature_segment, 1, False).reshape(N_DP * Q_DEV, NEG)
    rank_col = lax.dynamic_index_in_dim(ranks.reshape(N_DP, N_MP, Q_DEV, NEG), feature_segment, 1, False).reshape(N_DP * Q_DEV, NEG)
    eq, rq = normalize(jnp.dot(hq, weight, preferred_element_type=jnp.float32))
    ep, rp = normalize(jnp.dot(hp, weight, preferred_element_type=jnp.float32))
    eqb = eq.astype(jnp.bfloat16)
    epb = ep.astype(jnp.bfloat16).reshape(N_DP * P_DEV, PLEN, EMB)
    queries = N_DP * Q_DEV
    embedding_dimension = N_DP * P_DEV

    def score_one(block):
        expo, total = token_weights(eqb, block)
        return lax.optimization_barrier(jnp.sum((TAU * jnp.log(total)).reshape(queries, QLEN), axis=1))
    similarity_logits = lax.map(score_one, epb).T
    place = neg_col // P_DEV // N_MP * P_DEV + neg_col % P_DEV
    onehot = (place[:, :, None] == jnp.arange(embedding_dimension, dtype=jnp.int32)[None, None, :]).astype(jnp.float32)
    student = lax.optimization_barrier(jnp.sum(onehot * similarity_logits[:, None, :], axis=2))
    expo_s = jnp.exp(student)
    prob = expo_s / lax.optimization_barrier(jnp.sum(expo_s, axis=1, keepdims=True))
    teach = jnp.exp(-rank_col.astype(jnp.float32) / RANK_TEMP)
    teach = teach / lax.optimization_barrier(jnp.sum(teach, axis=1, keepdims=True))
    dscore = prob - teach
    dcol = lax.optimization_barrier(jnp.sum(onehot * dscore[:, :, None], axis=1))

    def back_one(acc, inputs):
        block, dcolumn = inputs
        expo, total = token_weights(eqb, block)
        share = jnp.repeat(dcolumn, QLEN) / total
        mixed = (expo * share[:, None]).astype(jnp.bfloat16)
        acc = acc + jnp.dot(mixed, block, preferred_element_type=jnp.float32)
        return (acc, jnp.dot(mixed.T, eqb, preferred_element_type=jnp.float32))
    deq, dep = lax.scan(back_one, jnp.zeros((queries * QLEN, EMB), jnp.float32), (epb, dcol.T))
    dep = dep.reshape(N_DP * p_rows, EMB)
    dvq = (rq * (deq - eq * lax.optimization_barrier(jnp.sum(eq * deq, axis=-1, keepdims=True)))).astype(jnp.bfloat16)
    dvp = (rp * (dep - ep * lax.optimization_barrier(jnp.sum(ep * dep, axis=-1, keepdims=True)))).astype(jnp.bfloat16)
    dhq = jnp.dot(dvq, weight.T, preferred_element_type=jnp.float32).astype(jnp.bfloat16)
    dw = jnp.dot(hq.T, dvq, preferred_element_type=jnp.float32) + jnp.dot(hp.T, dvp, preferred_element_type=jnp.float32)
    return (dhq.reshape(N_DP, q_rows, D), dw)

def reference(query_states, passage_states, proj_weight, negatives, ranks):

    def one(feature_segment):
        return column_grads(feature_segment, query_states, passage_states, proj_weight, negatives, ranks)
    dhq, dw = lax.map(one, jnp.arange(N_MP, dtype=jnp.int32))
    grad_queries = jnp.transpose(dhq, (1, 0, 2, 3)).reshape(NQUERIES * QLEN, D)
    return (grad_queries, lax.optimization_barrier(jnp.sum(dw, axis=0)))
```

```python
import functools

import jax
import jax.numpy as jnp
from jax import lax
from jax.experimental import pallas as pl
from jax.experimental.pallas import tpu as pltpu
from jax.sharding import Mesh
from jax.sharding import PartitionSpec as P

QLEN = 32
PLEN = 180
PROWS = 192
TAU = 0.1
RANK_TEMP = 8.0
EPS = 1e-06
LOG2E = 1.4426950408889634
F32 = jnp.float32
BF16 = jnp.bfloat16
MP = ("x", "y", "core")
ALL = ("dp", "x", "y", "core")


def contract(a, b, dims):
    return lax.dot_general(a, b, (dims, ((), ())), preferred_element_type=F32)


def lanes(shape):
    return lax.broadcasted_iota(jnp.int32, shape, 1)


def query_sums(x):
    width = x.shape[1]
    for s in (1, 2, 4, 8, 16):
        x = x + pltpu.roll(x, s, 1)
    x = jnp.where(lanes(x.shape) % QLEN == QLEN - 1, x, 0.0)
    for s in (1, 2, 4, 8, 16):
        x = x + pltpu.roll(x, width - s, 1)
    return x


def query_kernel(dp, n_mp, hq_ref, w_ref, neg_ref, rank_ref, tx_ref, vt_ref):
    held = 8
    vt = jnp.dot(hq_ref[...], w_ref[...], preferred_element_type=F32).T
    vt_ref[...] = vt
    et = vt * lax.rsqrt(jnp.sum(vt * vt, axis=0, keepdims=True) + EPS)
    etb = et.astype(BF16)
    neg = neg_ref[...]
    place = lax.div(neg, held * n_mp) * held + lax.rem(neg, held)
    teach = jnp.exp(-rank_ref[...].astype(F32) / RANK_TEMP)
    teach = teach / jnp.sum(teach, axis=1, keepdims=True)
    slots = dp * held
    row = lax.broadcasted_iota(jnp.int32, (slots, neg.shape[1]), 0)
    lane = lanes((slots, 128))
    table = jnp.zeros((slots, 128), F32)
    for q in range(neg.shape[0]):
        mine = jnp.where(place[q : q + 1, :] == row, teach[q : q + 1, :], 0.0)
        column = jnp.sum(mine, axis=1, keepdims=True)
        table = jnp.where(lane // QLEN == q, column, table)
    high = table.astype(BF16).astype(F32)
    low = table - high
    for d in range(dp):
        tx_ref[d, 0:128, :] = etb
        cut = slice(held * d, held * d + held)
        tx_ref[d, 128:144, :] = jnp.concatenate([high[cut], low[cut]], axis=0).astype(BF16)


def score_kernel(dp, hp_ref, w_ref, rx_ref, tx_ref, v_ref, expo_ref, sa_ref, sb_ref, ef, eb, lhs, sums):
    held = 8
    v_ref[...] = jnp.dot(hp_ref[...], w_ref[...], preferred_element_type=F32)
    row = lax.broadcasted_iota(jnp.int32, (16, PROWS), 0)
    col = lanes((16, PROWS))
    for p in range(held):
        v = v_ref[PLEN * p : PLEN * (p + 1), :]
        e = v * lax.rsqrt(jnp.sum(v * v, axis=1, keepdims=True) + EPS)
        ef[p, 176:256, :] = jnp.zeros((80, 128), F32)
        ef[p, 0:PLEN, :] = e
        padded = ef[p]
        eb[PROWS * p : PROWS * (p + 1), :] = padded[0:PROWS].astype(BF16)
        lhs[p, 0:128, :] = padded.T[:, 0:PROWS].astype(BF16)
        lhs[p, 128:144, :] = jnp.where((row == p) & (col < PLEN), 1.0, 0.0).astype(BF16)
    sums[...] = jnp.zeros((16, 128), F32)
    for j in range(dp // 2):
        pair = (2 * j, 2 * j + 1)
        wide = slice(256 * j, 256 * (j + 1))
        q = jnp.concatenate([rx_ref[k, 0:128, :] for k in pair], axis=1)
        codes = jnp.concatenate([rx_ref[k, 128:144, :].astype(F32) for k in pair], axis=1)
        teach = codes[0:8] + codes[8:16]
        listed = teach > 0.0
        dots = jnp.dot(eb[...], q, preferred_element_type=F32)
        expo = jnp.exp2(dots * (LOG2E / TAU)).astype(BF16)
        expo_ref[:, wide] = expo
        near = []
        total = None
        for p in range(held):
            out = jnp.dot(lhs[p], expo[PROWS * p : PROWS * (p + 1)], preferred_element_type=F32)
            near.append(out[0:128])
            total = out[128:136] if p == 0 else total + out[128:136]
        score = query_sums(TAU * jnp.log(total))
        es = jnp.where(listed, jnp.exp(score), 0.0)
        sa = es / total
        sb = teach / total
        sa_ref[:, wide] = sa
        sb_ref[:, wide] = sb
        a = near[0] * sa[0:1]
        b = near[0] * sb[0:1]
        for p in range(1, held):
            a = a + near[p] * sa[p : p + 1]
            b = b + near[p] * sb[p : p + 1]
        ab, bb = a.astype(BF16), b.astype(BF16)
        part = jnp.sum(es, axis=0, keepdims=True)
        for h, k in enumerate(pair):
            cut = slice(128 * h, 128 * (h + 1))
            tx_ref[k, 0:128, :] = ab[:, cut]
            tx_ref[k, 128:256, :] = bb[:, cut]
            sums[k : k + 1, :] = part[:, cut]
    whole = sums[...]
    high = whole.astype(BF16).astype(F32)
    rest = whole - high
    mid = rest.astype(BF16).astype(F32)
    low = rest - mid
    at = lanes((16, 128)) % QLEN
    coded = jnp.where(at == 0, high, jnp.where(at == 1, mid, jnp.where(at == 2, low, 0.0)))
    row16 = lax.broadcasted_iota(jnp.int32, (16, 128), 0)
    for d in range(dp):
        tx_ref[d, 256:272, :] = jnp.where(row16 == dp, coded[d : d + 1], coded).astype(BF16)


def grad_kernel(dp, hq_ref, hp_ref, w_ref, rx2_ref, rx_ref, vt_ref, v_ref, expo_ref, sa_ref, sb_ref, gq_ref, gw_ref, dv):
    held = 8
    part = rx_ref[0, 256:272, :].astype(F32)
    a = rx_ref[0, 0:128, :].astype(F32)
    b = rx_ref[0, 128:256, :].astype(F32)
    for s in range(1, dp):
        part = part + rx_ref[s, 256:272, :].astype(F32)
        a = a + rx_ref[s, 0:128, :].astype(F32)
        b = b + rx_ref[s, 128:256, :].astype(F32)
    sums = query_sums(part)
    inv = 1.0 / jnp.where(sums > 0.0, sums, 1.0)
    deq = a * inv[dp : dp + 1] - b
    vt = vt_ref[...]
    r = lax.rsqrt(jnp.sum(vt * vt, axis=0, keepdims=True) + EPS)
    et = vt * r
    dvq = (r * (deq - et * jnp.sum(et * deq, axis=0, keepdims=True))).astype(BF16)
    gq_ref[...] = contract(dvq, w_ref[...], ((0,), (1,))).astype(BF16)
    qt = jnp.concatenate([rx2_ref[k, 0:128, :] for k in range(dp)], axis=1).astype(F32)
    wide_inv = jnp.concatenate([inv[k : k + 1] for k in range(dp)], axis=1)
    share = sa_ref[...] * wide_inv - sb_ref[...]
    for p in range(held):
        scaled = (qt * share[p : p + 1]).astype(BF16)
        dep = contract(expo_ref[PROWS * p : PROWS * (p + 1), :], scaled, ((1,), (1,)))[0:PLEN]
        v = v_ref[PLEN * p : PLEN * (p + 1), :]
        rp = lax.rsqrt(jnp.sum(v * v, axis=1, keepdims=True) + EPS)
        e = v * rp
        dv[PLEN * p : PLEN * (p + 1), :] = rp * (dep - e * jnp.sum(e * dep, axis=1, keepdims=True))
    dvp = dv[...].astype(BF16)
    gwt = contract(dvp, hp_ref[...], ((0,), (0,))) + jnp.dot(dvq, hq_ref[...], preferred_element_type=F32)
    gw_ref[...] = gwt.T.astype(BF16)


def call(kernel, outs, scratch=()):
    return pl.pallas_call(
        kernel,
        out_shape=[jax.ShapeDtypeStruct(s, t) for s, t in outs],
        scratch_shapes=[pltpu.VMEM(s, t) for s, t in scratch],
        compiler_params=pltpu.CompilerParams(vmem_limit_bytes=48 * 1024 * 1024),
    )


def on_device(dp, n_mp, hq, hp, proj_weight, negatives, ranks):
    rows = proj_weight.shape[0]
    sent = jnp.broadcast_to(proj_weight[None], (n_mp,) + proj_weight.shape)
    weight = lax.all_to_all(sent, MP, 0, 0).reshape(n_mp * rows, 128)
    tx2, vt = call(
        functools.partial(query_kernel, dp, n_mp), [((dp, 144, 128), BF16), ((128, 128), F32)]
    )(hq, weight, negatives, ranks)
    rx2 = lax.all_to_all(tx2, "dp", 0, 0)
    n_q = dp * 128
    tx3, v, expo, sa, sb = call(
        functools.partial(score_kernel, dp),
        [
            ((dp, 272, 128), BF16),
            ((8 * PLEN, 128), F32),
            ((8 * PROWS, n_q), BF16),
            ((8, n_q), F32),
            ((8, n_q), F32),
        ],
        [((8, 256, 128), F32), ((8 * PROWS, 128), BF16), ((8, 144, PROWS), BF16), ((16, 128), F32)],
    )(hp, weight, rx2)
    rx3 = lax.all_to_all(tx3, "dp", 0, 0)
    grad_queries, gw = call(
        functools.partial(grad_kernel, dp),
        [((128, n_mp * rows), BF16), ((n_mp * rows, 128), BF16)],
        [((8 * PLEN, 128), F32)],
    )(hq, hp, weight, rx2, rx3, vt, v, expo, sa, sb)
    terms = lax.all_to_all(gw.reshape(n_mp, rows, 128), MP, 0, 0)
    mine = jnp.sum(terms.astype(F32), axis=0)
    shares = lax.all_to_all(jnp.broadcast_to(mine[None], (dp,) + mine.shape), "dp", 0, 0)
    return grad_queries, jnp.sum(shares, axis=0)


def solution(mesh):
    dp = mesh.shape["dp"]
    n_mp = mesh.shape["mp"]
    cut = (4, 8, 2) if n_mp == 64 else (n_mp, 1, 1)
    finer = Mesh(mesh.devices.reshape((dp,) + cut), ALL)
    placed = (P(ALL, None), P(ALL, None), P(MP, None), P(ALL, None), P(ALL, None))
    return jax.shard_map(
        functools.partial(on_device, dp, n_mp),
        mesh=finer,
        in_specs=placed,
        out_specs=(P(ALL, None), P(MP, None)),
        check_vma=False,
    )
```

```python
import functools

import jax
import jax.numpy as jnp
from jax import lax
from jax.experimental import pallas as pl
from jax.experimental.pallas import tpu as pltpu
from jax.sharding import Mesh
from jax.sharding import PartitionSpec as P

QLEN = 32
PLEN = 180
PROWS = 192
TAU = 0.1
RANK_TEMP = 8.0
EPS = 1e-06
LOG2E = 1.4426950408889634
F32 = jnp.float32
BF16 = jnp.bfloat16
MP = ("x", "y", "core")
ALL = ("dp", "x", "y", "core")


def contract(a, b, dims):
    return lax.dot_general(a, b, (dims, ((), ())), preferred_element_type=F32)


def lanes(shape):
    return lax.broadcasted_iota(jnp.int32, shape, 1)


def query_sums(x):
    width = x.shape[1]
    for s in (1, 2, 4, 8, 16):
        x = x + pltpu.roll(x, s, 1)
    x = jnp.where(lanes(x.shape) % QLEN == QLEN - 1, x, 0.0)
    for s in (1, 2, 4, 8, 16):
        x = x + pltpu.roll(x, width - s, 1)
    return x


def query_kernel(dp, n_mp, hq_hbm, w_ref, neg_hbm, rank_hbm, tx_ref, vt_ref, hq, neg_ref, rank_ref, sems):
    held = 8
    copies = [
        pltpu.make_async_copy(src, dst, sems.at[i])
        for i, (src, dst) in enumerate(((neg_hbm, neg_ref), (rank_hbm, rank_ref), (hq_hbm, hq)))
    ]
    for copy in copies:
        copy.start()
    copies[0].wait()
    copies[1].wait()
    neg = neg_ref[...]
    place = lax.div(neg, held * n_mp) * held + lax.rem(neg, held)
    teach = jnp.exp(-rank_ref[...].astype(F32) / RANK_TEMP)
    teach = teach / jnp.sum(teach, axis=1, keepdims=True)
    slots = dp * held
    row = lax.broadcasted_iota(jnp.int32, (slots, neg.shape[1]), 0)
    lane = lanes((slots, 128))
    table = jnp.zeros((slots, 128), F32)
    for q in range(neg.shape[0]):
        mine = jnp.where(place[q : q + 1, :] == row, teach[q : q + 1, :], 0.0)
        column = jnp.sum(mine, axis=1, keepdims=True)
        table = jnp.where(lane // QLEN == q, column, table)
    high = table.astype(BF16).astype(F32)
    low = table - high
    for d in range(dp):
        cut = slice(held * d, held * d + held)
        tx_ref[d, 128:144, :] = jnp.concatenate([high[cut], low[cut]], axis=0).astype(BF16)
    copies[2].wait()
    vt = jnp.dot(hq[...], w_ref[...], preferred_element_type=F32).T
    vt_ref[...] = vt
    et = vt * lax.rsqrt(jnp.sum(vt * vt, axis=0, keepdims=True) + EPS)
    etb = et.astype(BF16)
    for d in range(dp):
        tx_ref[d, 0:128, :] = etb


def score_kernel(
    dp, hp_hbm, w_ref, rx_ref, tx_ref, v_ref, expo_ref, sa_ref, sb_ref, a_ref, b_ref, hp, ef, eb, lhs, sums, sems
):
    held = 8
    parts = 3
    chunk = held * PLEN // parts
    copies = [
        pltpu.make_async_copy(
            hp_hbm.at[pl.ds(chunk * i, chunk)], hp.at[pl.ds(chunk * i, chunk)], sems.at[i]
        )
        for i in range(parts)
    ]
    for copy in copies:
        copy.start()
    row = lax.broadcasted_iota(jnp.int32, (16, PROWS), 0)
    col = lanes((16, PROWS))
    for p in range(held):
        lhs[p, 128:144, :] = jnp.where((row == p) & (col < PLEN), 1.0, 0.0).astype(BF16)
        ef[p, 176:256, :] = jnp.zeros((80, 128), F32)
    sums[...] = jnp.zeros((16, 128), F32)
    for i in range(parts):
        cut = slice(chunk * i, chunk * (i + 1))
        copies[i].wait()
        v_ref[cut, :] = jnp.dot(hp[cut, :], w_ref[...], preferred_element_type=F32)
    for p in range(held):
        v = v_ref[PLEN * p : PLEN * (p + 1), :]
        ef[p, 0:PLEN, :] = v * lax.rsqrt(jnp.sum(v * v, axis=1, keepdims=True) + EPS)
        padded = ef[p]
        eb[PROWS * p : PROWS * (p + 1), :] = padded[0:PROWS].astype(BF16)
        lhs[p, 0:128, :] = padded.T[:, 0:PROWS].astype(BF16)
    for j in range(dp // 2):
        pair = (2 * j, 2 * j + 1)
        wide = slice(256 * j, 256 * (j + 1))
        q = jnp.concatenate([rx_ref[k, 0:128, :] for k in pair], axis=1)
        codes = jnp.concatenate([rx_ref[k, 128:144, :].astype(F32) for k in pair], axis=1)
        teach = codes[0:8] + codes[8:16]
        listed = teach > 0.0
        dots = jnp.dot(eb[...], q, preferred_element_type=F32)
        expo = jnp.exp2(dots * (LOG2E / TAU)).astype(BF16)
        expo_ref[:, wide] = expo
        near = []
        total = None
        for p in range(held):
            out = jnp.dot(lhs[p], expo[PROWS * p : PROWS * (p + 1)], preferred_element_type=F32)
            near.append(out[0:128])
            total = out[128:136] if p == 0 else total + out[128:136]
        score = query_sums(TAU * jnp.log(total))
        es = jnp.where(listed, jnp.exp(score), 0.0)
        sa = es / total
        sb = teach / total
        sa_ref[:, wide] = sa
        sb_ref[:, wide] = sb
        a = near[0] * sa[0:1]
        b = near[0] * sb[0:1]
        for p in range(1, held):
            a = a + near[p] * sa[p : p + 1]
            b = b + near[p] * sb[p : p + 1]
        a_ref[:, wide] = a
        b_ref[:, wide] = b
        part = jnp.sum(es, axis=0, keepdims=True)
        for h, k in enumerate(pair):
            sums[k : k + 1, :] = part[:, 128 * h : 128 * (h + 1)]
    whole = sums[...]
    high = whole.astype(BF16).astype(F32)
    rest = whole - high
    mid = rest.astype(BF16).astype(F32)
    low = rest - mid
    at = lanes((16, 128)) % QLEN
    coded = jnp.where(at == 0, high, jnp.where(at == 1, mid, jnp.where(at == 2, low, 0.0)))
    for d in range(dp):
        tx_ref[d] = coded.astype(BF16)


def passage_kernel(dp, rx2_ref, rx_ref, v_ref, expo_ref, sa_ref, sb_ref, a_ref, b_ref, tx_ref, dv_ref, dv):
    held = 8
    part = rx_ref[0].astype(F32)
    for s in range(1, dp):
        part = part + rx_ref[s].astype(F32)
    sums = query_sums(part)
    inv = 1.0 / jnp.where(sums > 0.0, sums, 1.0)
    for k in range(dp):
        cut = slice(128 * k, 128 * (k + 1))
        tx_ref[k] = (a_ref[:, cut] * inv[k : k + 1] - b_ref[:, cut]).astype(BF16)
    qt = jnp.concatenate([rx2_ref[k, 0:128, :] for k in range(dp)], axis=1).astype(F32)
    wide_inv = jnp.concatenate([inv[k : k + 1] for k in range(dp)], axis=1)
    share = sa_ref[...] * wide_inv - sb_ref[...]
    for p in range(held):
        scaled = (qt * share[p : p + 1]).astype(BF16)
        dep = contract(expo_ref[PROWS * p : PROWS * (p + 1), :], scaled, ((1,), (1,)))[0:PLEN]
        v = v_ref[PLEN * p : PLEN * (p + 1), :]
        rp = lax.rsqrt(jnp.sum(v * v, axis=1, keepdims=True) + EPS)
        e = v * rp
        dv[PLEN * p : PLEN * (p + 1), :] = rp * (dep - e * jnp.sum(e * dep, axis=1, keepdims=True))
    dv_ref[...] = dv[...].astype(BF16)


def grad_kernel(dp, hq_ref, hp_ref, w_ref, rx_ref, vt_ref, dvp_ref, gq_ref, gw_ref):
    deq = rx_ref[0].astype(F32)
    for s in range(1, dp):
        deq = deq + rx_ref[s].astype(F32)
    vt = vt_ref[...]
    r = lax.rsqrt(jnp.sum(vt * vt, axis=0, keepdims=True) + EPS)
    et = vt * r
    dvq = (r * (deq - et * jnp.sum(et * deq, axis=0, keepdims=True))).astype(BF16)
    gq_ref[...] = contract(dvq, w_ref[...], ((0,), (1,))).astype(BF16)
    gwt = contract(dvp_ref[...], hp_ref[...], ((0,), (0,)))
    gwt = gwt + jnp.dot(dvq, hq_ref[...], preferred_element_type=F32)
    gw_ref[...] = gwt.T.astype(BF16)


def call(kernel, outs, scratch=(), far=(), n_in=0, mib=20):
    specs = [pl.BlockSpec(memory_space=pltpu.HBM if i in far else pltpu.VMEM) for i in range(n_in)]
    return pl.pallas_call(
        kernel,
        out_shape=[jax.ShapeDtypeStruct(s, t) for s, t in outs],
        in_specs=specs,
        scratch_shapes=[pltpu.VMEM(*s) if isinstance(s, tuple) else s for s in scratch],
        compiler_params=pltpu.CompilerParams(vmem_limit_bytes=mib * 1024 * 1024),
    )


def on_device(dp, n_mp, hq, hp, proj_weight, negatives, ranks):
    rows = proj_weight.shape[0]
    width = n_mp * rows
    n_q = dp * 128
    n_p = 8 * PLEN
    sent = jnp.broadcast_to(proj_weight[None], (n_mp,) + proj_weight.shape)
    weight = lax.all_to_all(sent, MP, 0, 0).reshape(width, 128)
    tx2, vt = call(
        functools.partial(query_kernel, dp, n_mp),
        [((dp, 144, 128), BF16), ((128, 128), F32)],
        [
            (hq.shape, BF16),
            (negatives.shape, jnp.int32),
            (ranks.shape, jnp.int32),
            pltpu.SemaphoreType.DMA((3,)),
        ],
        far=(0, 2, 3),
        n_in=4,
    )(hq, weight, negatives, ranks)
    rx2 = lax.all_to_all(tx2, "dp", 0, 0)
    tx3, v, expo, sa, sb, a, b = call(
        functools.partial(score_kernel, dp),
        [
            ((dp, 16, 128), BF16),
            ((n_p, 128), F32),
            ((8 * PROWS, n_q), BF16),
            ((8, n_q), F32),
            ((8, n_q), F32),
            ((128, n_q), F32),
            ((128, n_q), F32),
        ],
        [
            (hp.shape, BF16),
            ((8, 256, 128), F32),
            ((8 * PROWS, 128), BF16),
            ((8, 144, PROWS), BF16),
            ((16, 128), F32),
            pltpu.SemaphoreType.DMA((3,)),
        ],
        far=(0,),
        n_in=3,
    )(hp, weight, rx2)
    rx3 = lax.all_to_all(tx3, "dp", 0, 0)
    tx4, dvp = call(
        functools.partial(passage_kernel, dp),
        [((dp, 128, 128), BF16), ((n_p, 128), BF16)],
        [((n_p, 128), F32)],
        n_in=8,
    )(rx2, rx3, v, expo, sa, sb, a, b)
    rx4 = lax.all_to_all(tx4, "dp", 0, 0)
    grad_queries, gw = call(
        functools.partial(grad_kernel, dp), [((128, width), BF16), ((width, 128), BF16)], n_in=6
    )(hq, hp, weight, rx4, vt, dvp)
    terms = lax.all_to_all(gw.reshape(n_mp, rows, 128), MP, 0, 0)
    mine = jnp.sum(terms.astype(F32), axis=0)
    shares = lax.all_to_all(jnp.broadcast_to(mine[None], (dp,) + mine.shape), "dp", 0, 0)
    return grad_queries, jnp.sum(shares, axis=0)


def solution(mesh):
    dp = mesh.shape["dp"]
    n_mp = mesh.shape["mp"]
    cut = (4, 8, 2) if n_mp == 64 else (n_mp, 1, 1)
    finer = Mesh(mesh.devices.reshape((dp,) + cut), ALL)
    placed = (P(ALL, None), P(ALL, None), P(MP, None), P(ALL, None), P(ALL, None))
    return jax.shard_map(
        functools.partial(on_device, dp, n_mp),
        mesh=finer,
        in_specs=placed,
        out_specs=(P(ALL, None), P(MP, None)),
        check_vma=False,
    )
```

```python
import functools

import jax
import jax.numpy as jnp
from jax import lax
from jax.experimental import pallas as pl
from jax.experimental.pallas import tpu as pltpu
from jax.sharding import Mesh
from jax.sharding import PartitionSpec as P

QLEN = 32
PLEN = 180
PROWS = 192
TAU = 0.1
RANK_TEMP = 8.0
EPS = 1e-06
LOG2E = 1.4426950408889634
F32 = jnp.float32
BF16 = jnp.bfloat16
MP = ("x", "y", "core")
ALL = ("dp", "x", "y", "core")


def contract(a, b, dims):
    return lax.dot_general(a, b, (dims, ((), ())), preferred_element_type=F32)


def lanes(shape):
    return lax.broadcasted_iota(jnp.int32, shape, 1)


def query_sums(x):
    width = x.shape[1]
    for s in (1, 2, 4, 8, 16):
        x = x + pltpu.roll(x, s, 1)
    x = jnp.where(lanes(x.shape) % QLEN == QLEN - 1, x, 0.0)
    for s in (1, 2, 4, 8, 16):
        x = x + pltpu.roll(x, width - s, 1)
    return x


def copies_kernel(w_ref, out_ref):
    for i in range(out_ref.shape[0]):
        out_ref[i] = w_ref[...]


def query_kernel(dp, n_mp, hq_ref, w_ref, neg_ref, rank_ref, tx_ref, vt_ref):
    held = 8
    neg = neg_ref[...]
    place = lax.div(neg, held * n_mp) * held + lax.rem(neg, held)
    teach = jnp.exp(-rank_ref[...].astype(F32) / RANK_TEMP)
    teach = teach / jnp.sum(teach, axis=1, keepdims=True)
    slots = dp * held
    row = lax.broadcasted_iota(jnp.int32, (slots, neg.shape[1]), 0)
    lane = lanes((slots, 128))
    table = jnp.zeros((slots, 128), F32)
    for q in range(neg.shape[0]):
        mine = jnp.where(place[q : q + 1, :] == row, teach[q : q + 1, :], 0.0)
        column = jnp.sum(mine, axis=1, keepdims=True)
        table = jnp.where(lane // QLEN == q, column, table)
    high = table.astype(BF16).astype(F32)
    low = table - high
    for d in range(dp):
        cut = slice(held * d, held * d + held)
        tx_ref[d, 128:144, :] = jnp.concatenate([high[cut], low[cut]], axis=0).astype(BF16)
    vt = jnp.dot(hq_ref[...], w_ref[...], preferred_element_type=F32).T
    vt_ref[...] = vt
    et = vt * lax.rsqrt(jnp.sum(vt * vt, axis=0, keepdims=True) + EPS)
    etb = et.astype(BF16)
    for d in range(dp):
        tx_ref[d, 0:128, :] = etb


def score_kernel(dp, hp_ref, w_ref, rx_ref, tx_ref, v_ref, expo_ref, sa_ref, sb_ref, a_ref, b_ref, ef, eb, lhs, sums):
    held = 8
    v_ref[...] = jnp.dot(hp_ref[...], w_ref[...], preferred_element_type=F32)
    row = lax.broadcasted_iota(jnp.int32, (16, PROWS), 0)
    col = lanes((16, PROWS))
    for p in range(held):
        lhs[p, 128:144, :] = jnp.where((row == p) & (col < PLEN), 1.0, 0.0).astype(BF16)
        ef[p, 176:256, :] = jnp.zeros((80, 128), F32)
    sums[...] = jnp.zeros((16, 128), F32)
    for p in range(held):
        v = v_ref[PLEN * p : PLEN * (p + 1), :]
        ef[p, 0:PLEN, :] = v * lax.rsqrt(jnp.sum(v * v, axis=1, keepdims=True) + EPS)
        padded = ef[p]
        eb[PROWS * p : PROWS * (p + 1), :] = padded[0:PROWS].astype(BF16)
        lhs[p, 0:128, :] = padded.T[:, 0:PROWS].astype(BF16)
    for j in range(dp // 4):
        pair = (4 * j, 4 * j + 1, 4 * j + 2, 4 * j + 3)
        wide = slice(512 * j, 512 * (j + 1))
        q = jnp.concatenate([rx_ref[k, 0:128, :] for k in pair], axis=1)
        codes = jnp.concatenate([rx_ref[k, 128:144, :].astype(F32) for k in pair], axis=1)
        teach = codes[0:8] + codes[8:16]
        listed = teach > 0.0
        dots = jnp.dot(eb[...], q, preferred_element_type=F32)
        expo = jnp.exp2(dots * (LOG2E / TAU)).astype(BF16)
        expo_ref[:, wide] = expo
        near = []
        total = None
        for p in range(held):
            out = jnp.dot(lhs[p], expo[PROWS * p : PROWS * (p + 1)], preferred_element_type=F32)
            near.append(out[0:128])
            total = out[128:136] if p == 0 else total + out[128:136]
        score = query_sums(TAU * jnp.log(total))
        es = jnp.where(listed, jnp.exp(score), 0.0)
        sa = es / total
        sb = teach / total
        sa_ref[:, wide] = sa
        sb_ref[:, wide] = sb
        a = near[0] * sa[0:1]
        b = near[0] * sb[0:1]
        for p in range(1, held):
            a = a + near[p] * sa[p : p + 1]
            b = b + near[p] * sb[p : p + 1]
        a_ref[:, wide] = a
        b_ref[:, wide] = b
        part = jnp.sum(es, axis=0, keepdims=True)
        for h, k in enumerate(pair):
            sums[k : k + 1, :] = part[:, 128 * h : 128 * (h + 1)]
    whole = sums[...]
    high = whole.astype(BF16).astype(F32)
    rest = whole - high
    mid = rest.astype(BF16).astype(F32)
    low = rest - mid
    at = lanes((16, 128)) % QLEN
    coded = jnp.where(at == 0, high, jnp.where(at == 1, mid, jnp.where(at == 2, low, 0.0)))
    for d in range(dp):
        tx_ref[d] = coded.astype(BF16)


def passage_kernel(dp, rx2_ref, rx_ref, v_ref, expo_ref, sa_ref, sb_ref, a_ref, b_ref, tx_ref, dv_ref, dv):
    held = 8
    part = rx_ref[0].astype(F32)
    for s in range(1, dp):
        part = part + rx_ref[s].astype(F32)
    sums = query_sums(part)
    inv = 1.0 / jnp.where(sums > 0.0, sums, 1.0)
    for k in range(dp):
        cut = slice(128 * k, 128 * (k + 1))
        tx_ref[k] = (a_ref[:, cut] * inv[k : k + 1] - b_ref[:, cut]).astype(BF16)
    qt = jnp.concatenate([rx2_ref[k, 0:128, :] for k in range(dp)], axis=1).astype(F32)
    wide_inv = jnp.concatenate([inv[k : k + 1] for k in range(dp)], axis=1)
    share = sa_ref[...] * wide_inv - sb_ref[...]
    for p in range(held):
        scaled = (qt * share[p : p + 1]).astype(BF16)
        dep = contract(expo_ref[PROWS * p : PROWS * (p + 1), :], scaled, ((1,), (1,)))[0:PLEN]
        v = v_ref[PLEN * p : PLEN * (p + 1), :]
        rp = lax.rsqrt(jnp.sum(v * v, axis=1, keepdims=True) + EPS)
        e = v * rp
        dv[PLEN * p : PLEN * (p + 1), :] = rp * (dep - e * jnp.sum(e * dep, axis=1, keepdims=True))
    dv_ref[...] = dv[...].astype(BF16)


def grad_kernel(dp, hq_ref, hp_ref, w_ref, rx_ref, vt_ref, dvp_ref, gq_ref, gw_ref):
    deq = rx_ref[0].astype(F32)
    for s in range(1, dp):
        deq = deq + rx_ref[s].astype(F32)
    vt = vt_ref[...]
    r = lax.rsqrt(jnp.sum(vt * vt, axis=0, keepdims=True) + EPS)
    et = vt * r
    dvq = (r * (deq - et * jnp.sum(et * deq, axis=0, keepdims=True))).astype(BF16)
    gq_ref[...] = contract(dvq, w_ref[...], ((0,), (1,))).astype(BF16)
    gwt = contract(dvp_ref[...], hp_ref[...], ((0,), (0,)))
    gwt = gwt + jnp.dot(dvq, hq_ref[...], preferred_element_type=F32)
    gw_ref[...] = gwt.T.astype(BF16)


def call(kernel, outs, scratch=(), mib=20, gflop=0):
    return pl.pallas_call(
        kernel,
        out_shape=[jax.ShapeDtypeStruct(s, t) for s, t in outs],
        scratch_shapes=[pltpu.VMEM(*s) if isinstance(s, tuple) else s for s in scratch],
        cost_estimate=pl.CostEstimate(flops=gflop * 10**9, bytes_accessed=4 * 10**6, transcendentals=0),
        compiler_params=pltpu.CompilerParams(vmem_limit_bytes=mib * 1024 * 1024),
    )


def on_device(dp, n_mp, hq, hp, proj_weight, negatives, ranks):
    rows = proj_weight.shape[0]
    width = n_mp * rows
    n_q = dp * 128
    n_p = 8 * PLEN
    (sent,) = call(copies_kernel, [((n_mp,) + proj_weight.shape, BF16)], gflop=8)(proj_weight)
    weight = lax.all_to_all(sent, MP, 0, 0).reshape(width, 128)
    tx2, vt = call(
        functools.partial(query_kernel, dp, n_mp), [((dp, 144, 128), BF16), ((128, 128), F32)], gflop=4
    )(hq, weight, negatives, ranks)
    rx2 = lax.all_to_all(tx2, "dp", 0, 0)
    tx3, v, expo, sa, sb, a, b = call(
        functools.partial(score_kernel, dp),
        [
            ((dp, 16, 128), BF16),
            ((n_p, 128), F32),
            ((8 * PROWS, n_q), BF16),
            ((8, n_q), F32),
            ((8, n_q), F32),
            ((128, n_q), F32),
            ((128, n_q), F32),
        ],
        [((8, 256, 128), F32), ((8 * PROWS, 128), BF16), ((8, 144, PROWS), BF16), ((16, 128), F32)],
        gflop=2,
    )(hp, weight, rx2)
    rx3 = lax.all_to_all(tx3, "dp", 0, 0)
    tx4, dvp = call(
        functools.partial(passage_kernel, dp),
        [((dp, 128, 128), BF16), ((n_p, 128), BF16)],
        [((n_p, 128), F32)],
        gflop=1,
    )(rx2, rx3, v, expo, sa, sb, a, b)
    rx4 = lax.all_to_all(tx4, "dp", 0, 0)
    grad_queries, gw = call(
        functools.partial(grad_kernel, dp), [((128, width), BF16), ((width, 128), BF16)], gflop=1
    )(hq, hp, weight, rx4, vt, dvp)
    terms = lax.all_to_all(gw.reshape(n_mp, rows, 128), MP, 0, 0)
    mine = jnp.sum(terms.astype(F32), axis=0)
    shares = lax.all_to_all(jnp.broadcast_to(mine[None], (dp,) + mine.shape), "dp", 0, 0)
    return grad_queries, jnp.sum(shares, axis=0)


def solution(mesh):
    dp = mesh.shape["dp"]
    n_mp = mesh.shape["mp"]
    cut = (4, 8, 2) if n_mp == 64 else (n_mp, 1, 1)
    finer = Mesh(mesh.devices.reshape((dp,) + cut), ALL)
    placed = (P(ALL, None), P(ALL, None), P(MP, None), P(ALL, None), P(ALL, None))
    return jax.shard_map(
        functools.partial(on_device, dp, n_mp),
        mesh=finer,
        in_specs=placed,
        out_specs=(P(ALL, None), P(MP, None)),
        check_vma=False,
    )
```

```python
import functools

import jax
import jax.numpy as jnp
from jax import lax
from jax.experimental import pallas as pl
from jax.experimental.pallas import tpu as pltpu
from jax.sharding import Mesh
from jax.sharding import PartitionSpec as P

QLEN = 32
PLEN = 180
PROWS = 192
TAU = 0.1
RANK_TEMP = 8.0
EPS = 1e-06
LOG2E = 1.4426950408889634
F32 = jnp.float32
BF16 = jnp.bfloat16
MP = ("x", "y", "core")
ALL = ("dp", "x", "y", "core")


def contract(a, b, dims):
    return lax.dot_general(a, b, (dims, ((), ())), preferred_element_type=F32)


def lanes(shape):
    return lax.broadcasted_iota(jnp.int32, shape, 1)


def query_sums(x):
    width = x.shape[1]
    for s in (1, 2, 4, 8, 16):
        x = x + pltpu.roll(x, s, 1)
    x = jnp.where(lanes(x.shape) % QLEN == QLEN - 1, x, 0.0)
    for s in (1, 2, 4, 8, 16):
        x = x + pltpu.roll(x, width - s, 1)
    return x


def copies_kernel(w_ref, out_ref):
    for i in range(out_ref.shape[0]):
        out_ref[i] = w_ref[...]


def query_kernel(dp, n_mp, hq_ref, w_ref, neg_ref, rank_ref, tx_ref, vt_ref):
    held = 8
    neg = neg_ref[...]
    place = lax.div(neg, held * n_mp) * held + lax.rem(neg, held)
    teach = jnp.exp(-rank_ref[...].astype(F32) / RANK_TEMP)
    teach = teach / jnp.sum(teach, axis=1, keepdims=True)
    slots = dp * held
    row = lax.broadcasted_iota(jnp.int32, (slots, neg.shape[1]), 0)
    lane = lanes((slots, 128))
    table = jnp.zeros((slots, 128), F32)
    for q in range(neg.shape[0]):
        mine = jnp.where(place[q : q + 1, :] == row, teach[q : q + 1, :], 0.0)
        column = jnp.sum(mine, axis=1, keepdims=True)
        table = jnp.where(lane // QLEN == q, column, table)
    high = table.astype(BF16).astype(F32)
    low = table - high
    for d in range(dp):
        cut = slice(held * d, held * d + held)
        tx_ref[d, 128:144, :] = jnp.concatenate([high[cut], low[cut]], axis=0).astype(BF16)
    vt = jnp.dot(hq_ref[...], w_ref[...], preferred_element_type=F32).T
    vt_ref[...] = vt
    et = vt * lax.rsqrt(jnp.sum(vt * vt, axis=0, keepdims=True) + EPS)
    etb = et.astype(BF16)
    for d in range(dp):
        tx_ref[d, 0:128, :] = etb


def score_kernel(dp, hp_ref, w_ref, rx_ref, tx_ref, v_ref, eb_ref, expo_ref, sa_ref, sb_ref, ef, sums):
    held = 8
    v_ref[...] = jnp.dot(hp_ref[...], w_ref[...], preferred_element_type=F32)
    for p in range(held):
        v = v_ref[PLEN * p : PLEN * (p + 1), :]
        ef[PROWS * (p + 1) - 16 : PROWS * (p + 1), :] = jnp.zeros((16, 128), F32)
        ef[PROWS * p : PROWS * p + PLEN, :] = v * lax.rsqrt(jnp.sum(v * v, axis=1, keepdims=True) + EPS)
    eb_ref[...] = ef[...].astype(BF16)
    q = jnp.concatenate([rx_ref[k, 0:128, :] for k in range(dp)], axis=1)
    codes = jnp.concatenate([rx_ref[k, 128:144, :].astype(F32) for k in range(dp)], axis=1)
    teach = codes[0:8] + codes[8:16]
    dots = jnp.dot(eb_ref[...], q, preferred_element_type=F32)
    row = lax.broadcasted_iota(jnp.int32, (8, 128 * dp), 0)
    total = jnp.zeros((8, 128 * dp), F32)
    for p in range(held):
        cut = slice(PROWS * p, PROWS * (p + 1))
        expo = jnp.exp2(dots[cut] * (LOG2E / TAU))
        expo_ref[cut, :] = expo.astype(BF16)
        part = jnp.where(row < PLEN - 176, expo[176:184], 0.0)
        for i in range(22):
            part = part + expo[8 * i : 8 * (i + 1)]
        total = jnp.where(row == p, jnp.sum(part, axis=0, keepdims=True), total)
    score = query_sums(TAU * jnp.log(total))
    es = jnp.where(teach > 0.0, jnp.exp(score), 0.0)
    sa_ref[...] = es / total
    sb_ref[...] = teach / total
    listed = jnp.sum(es, axis=0, keepdims=True)
    sums[...] = jnp.zeros((16, 128), F32)
    for k in range(dp):
        sums[k : k + 1, :] = listed[:, 128 * k : 128 * (k + 1)]
    whole = sums[...]
    high = whole.astype(BF16).astype(F32)
    rest = whole - high
    mid = rest.astype(BF16).astype(F32)
    low = rest - mid
    at = lanes((16, 128)) % QLEN
    coded = jnp.where(at == 0, high, jnp.where(at == 1, mid, jnp.where(at == 2, low, 0.0)))
    for d in range(dp):
        tx_ref[d] = coded.astype(BF16)


def passage_kernel(dp, rx2_ref, rx_ref, v_ref, eb_ref, expo_ref, sa_ref, sb_ref, tx_ref, dv_ref, mixed, dv):
    held = 8
    part = rx_ref[0].astype(F32)
    for s in range(1, dp):
        part = part + rx_ref[s].astype(F32)
    sums = query_sums(part)
    inv = 1.0 / jnp.where(sums > 0.0, sums, 1.0)
    wide_inv = jnp.concatenate([inv[k : k + 1] for k in range(dp)], axis=1)
    share = sa_ref[...] * wide_inv - sb_ref[...]
    for p in range(held):
        cut = slice(PROWS * p, PROWS * (p + 1))
        mixed[cut, :] = (expo_ref[cut, :].astype(F32) * share[p : p + 1]).astype(BF16)
    deq = contract(eb_ref[...], mixed[...], ((0,), (0,))).astype(BF16)
    for k in range(dp):
        tx_ref[k] = deq[:, 128 * k : 128 * (k + 1)]
    qt = jnp.concatenate([rx2_ref[k, 0:128, :] for k in range(dp)], axis=1)
    for p in range(held):
        dep = contract(mixed[PROWS * p : PROWS * (p + 1), :], qt, ((1,), (1,)))[0:PLEN]
        v = v_ref[PLEN * p : PLEN * (p + 1), :]
        rp = lax.rsqrt(jnp.sum(v * v, axis=1, keepdims=True) + EPS)
        e = v * rp
        dv[PLEN * p : PLEN * (p + 1), :] = rp * (dep - e * jnp.sum(e * dep, axis=1, keepdims=True))
    dv_ref[...] = dv[...].astype(BF16)


def grad_kernel(dp, hq_ref, hp_ref, w_ref, rx_ref, vt_ref, dvp_ref, gq_ref, gw_ref):
    deq = rx_ref[0].astype(F32)
    for s in range(1, dp):
        deq = deq + rx_ref[s].astype(F32)
    vt = vt_ref[...]
    r = lax.rsqrt(jnp.sum(vt * vt, axis=0, keepdims=True) + EPS)
    et = vt * r
    dvq = (r * (deq - et * jnp.sum(et * deq, axis=0, keepdims=True))).astype(BF16)
    gq_ref[...] = contract(dvq, w_ref[...], ((0,), (1,))).astype(BF16)
    gwt = contract(dvp_ref[...], hp_ref[...], ((0,), (0,)))
    gwt = gwt + jnp.dot(dvq, hq_ref[...], preferred_element_type=F32)
    gw_ref[...] = gwt.T.astype(BF16)


def share_kernel(terms_ref, tx_ref):
    mine = terms_ref[0].astype(F32)
    for m in range(1, terms_ref.shape[0]):
        mine = mine + terms_ref[m].astype(F32)
    for d in range(tx_ref.shape[0]):
        tx_ref[d] = mine


def sum_kernel(shares_ref, out_ref):
    total = shares_ref[0]
    for d in range(1, shares_ref.shape[0]):
        total = total + shares_ref[d]
    out_ref[...] = total


def call(kernel, outs, scratch=(), mib=20, gflop=0):
    return pl.pallas_call(
        kernel,
        out_shape=[jax.ShapeDtypeStruct(s, t) for s, t in outs],
        scratch_shapes=[pltpu.VMEM(*s) if isinstance(s, tuple) else s for s in scratch],
        cost_estimate=pl.CostEstimate(flops=gflop * 10**9, bytes_accessed=4 * 10**6, transcendentals=0),
        compiler_params=pltpu.CompilerParams(vmem_limit_bytes=mib * 1024 * 1024),
    )


def on_device(dp, n_mp, hq, hp, proj_weight, negatives, ranks):
    rows = proj_weight.shape[0]
    width = n_mp * rows
    n_q = dp * 128
    n_p = 8 * PLEN
    (sent,) = call(copies_kernel, [((n_mp,) + proj_weight.shape, BF16)], gflop=8)(proj_weight)
    weight = lax.all_to_all(sent, MP, 0, 0).reshape(width, 128)
    tx2, vt = call(
        functools.partial(query_kernel, dp, n_mp), [((dp, 144, 128), BF16), ((128, 128), F32)], gflop=4
    )(hq, weight, negatives, ranks)
    rx2 = lax.all_to_all(tx2, "dp", 0, 0)
    tx3, v, eb, expo, sa, sb = call(
        functools.partial(score_kernel, dp),
        [
            ((dp, 16, 128), BF16),
            ((n_p, 128), F32),
            ((8 * PROWS, 128), BF16),
            ((8 * PROWS, n_q), BF16),
            ((8, n_q), F32),
            ((8, n_q), F32),
        ],
        [((8 * PROWS, 128), F32), ((16, 128), F32)],
        mib=28,
        gflop=2,
    )(hp, weight, rx2)
    rx3 = lax.all_to_all(tx3, "dp", 0, 0)
    tx4, dvp = call(
        functools.partial(passage_kernel, dp),
        [((dp, 128, 128), BF16), ((n_p, 128), BF16)],
        [((8 * PROWS, n_q), BF16), ((n_p, 128), F32)],
        gflop=1,
    )(rx2, rx3, v, eb, expo, sa, sb)
    rx4 = lax.all_to_all(tx4, "dp", 0, 0)
    grad_queries, gw = call(
        functools.partial(grad_kernel, dp), [((128, width), BF16), ((width, 128), BF16)], gflop=1
    )(hq, hp, weight, rx4, vt, dvp)
    terms = lax.all_to_all(gw.reshape(n_mp, rows, 128), MP, 0, 0)
    (tx5,) = call(share_kernel, [((dp, rows, 128), F32)])(terms)
    shares = lax.all_to_all(tx5, "dp", 0, 0)
    (grad_weight,) = call(sum_kernel, [((rows, 128), F32)])(shares)
    return grad_queries, grad_weight


def solution(mesh):
    dp = mesh.shape["dp"]
    n_mp = mesh.shape["mp"]
    cut = (4, 8, 2) if n_mp == 64 else (n_mp, 1, 1)
    finer = Mesh(mesh.devices.reshape((dp,) + cut), ALL)
    placed = (P(ALL, None), P(ALL, None), P(MP, None), P(ALL, None), P(ALL, None))
    return jax.shard_map(
        functools.partial(on_device, dp, n_mp),
        mesh=finer,
        in_specs=placed,
        out_specs=(P(ALL, None), P(MP, None)),
        check_vma=False,
    )
```

```python
import functools

import jax
import jax.numpy as jnp
from jax import lax
from jax.experimental import pallas as pl
from jax.experimental.pallas import tpu as pltpu
from jax.sharding import Mesh
from jax.sharding import PartitionSpec as P

QLEN = 32
PLEN = 180
PROWS = 192
TAU = 0.1
RANK_TEMP = 8.0
EPS = 1e-06
LOG2E = 1.4426950408889634
F32 = jnp.float32
BF16 = jnp.bfloat16
MP = ("x", "y", "core")
ALL = ("dp", "x", "y", "core")


def contract(a, b, dims):
    return lax.dot_general(a, b, (dims, ((), ())), preferred_element_type=F32)


def lanes(shape):
    return lax.broadcasted_iota(jnp.int32, shape, 1)


def query_sums(x):
    width = x.shape[1]
    for s in (1, 2, 4, 8, 16):
        x = x + pltpu.roll(x, s, 1)
    x = jnp.where(lanes(x.shape) % QLEN == QLEN - 1, x, 0.0)
    for s in (1, 2, 4, 8, 16):
        x = x + pltpu.roll(x, width - s, 1)
    return x


def copies_kernel(w_ref, out_ref):
    for i in range(out_ref.shape[0]):
        out_ref[i] = w_ref[...]


def query_kernel(dp, n_mp, hq_ref, w_ref, neg_ref, rank_ref, tx_ref, vt_ref):
    held = 8
    neg = neg_ref[...]
    place = lax.div(neg, held * n_mp) * held + lax.rem(neg, held)
    teach = jnp.exp(-rank_ref[...].astype(F32) / RANK_TEMP)
    teach = teach / jnp.sum(teach, axis=1, keepdims=True)
    slots = dp * held
    row = lax.broadcasted_iota(jnp.int32, (slots, neg.shape[1]), 0)
    lane = lanes((slots, 128))
    table = jnp.zeros((slots, 128), F32)
    for q in range(neg.shape[0]):
        mine = jnp.where(place[q : q + 1, :] == row, teach[q : q + 1, :], 0.0)
        column = jnp.sum(mine, axis=1, keepdims=True)
        table = jnp.where(lane // QLEN == q, column, table)
    high = table.astype(BF16).astype(F32)
    halves = jnp.where(lane % QLEN < QLEN // 2, high, table - high)
    for d in range(dp):
        tx_ref[d, 128:136, :] = halves[held * d : held * d + held].astype(BF16)
    vt = jnp.dot(hq_ref[...], w_ref[...], preferred_element_type=F32).T
    vt_ref[...] = vt
    et = vt * lax.rsqrt(jnp.sum(vt * vt, axis=0, keepdims=True) + EPS)
    etb = et.astype(BF16)
    for d in range(dp):
        tx_ref[d, 0:128, :] = etb


def score_kernel(dp, hp_ref, w_ref, rx_ref, tx_ref, v_ref, eb_ref, expo_ref, sa_ref, sb_ref, ef, sums):
    held = 8
    v_ref[...] = jnp.dot(hp_ref[...], w_ref[...], preferred_element_type=F32)
    for p in range(held):
        v = v_ref[PLEN * p : PLEN * (p + 1), :]
        ef[PROWS * (p + 1) - 16 : PROWS * (p + 1), :] = jnp.zeros((16, 128), F32)
        ef[PROWS * p : PROWS * p + PLEN, :] = v * lax.rsqrt(jnp.sum(v * v, axis=1, keepdims=True) + EPS)
    eb_ref[...] = ef[...].astype(BF16)
    q = jnp.concatenate([rx_ref[k, 0:128, :] for k in range(dp)], axis=1)
    codes = jnp.concatenate([rx_ref[k, 128:136, :].astype(F32) for k in range(dp)], axis=1)
    half = QLEN // 2
    other = jnp.where(
        lanes(codes.shape) % QLEN < half, pltpu.roll(codes, 128 * dp - half, 1), pltpu.roll(codes, half, 1)
    )
    teach = codes + other
    dots = jnp.dot(eb_ref[...], q, preferred_element_type=F32)
    row = lax.broadcasted_iota(jnp.int32, (8, 128 * dp), 0)
    total = jnp.zeros((8, 128 * dp), F32)
    for p in range(held):
        cut = slice(PROWS * p, PROWS * (p + 1))
        expo = jnp.exp2(dots[cut] * (LOG2E / TAU))
        expo_ref[cut, :] = expo.astype(BF16)
        part = jnp.where(row < PLEN - 176, expo[176:184], 0.0)
        for i in range(22):
            part = part + expo[8 * i : 8 * (i + 1)]
        total = jnp.where(row == p, jnp.sum(part, axis=0, keepdims=True), total)
    score = query_sums(TAU * jnp.log(total))
    es = jnp.where(teach > 0.0, jnp.exp(score), 0.0)
    sa_ref[...] = es / total
    sb_ref[...] = teach / total
    listed = jnp.sum(es, axis=0, keepdims=True)
    sums[...] = jnp.zeros((16, 128), F32)
    for k in range(dp):
        sums[k : k + 1, :] = listed[:, 128 * k : 128 * (k + 1)]
    whole = sums[...]
    high = whole.astype(BF16).astype(F32)
    rest = whole - high
    mid = rest.astype(BF16).astype(F32)
    low = rest - mid
    at = lanes((16, 128)) % QLEN
    coded = jnp.where(at == 0, high, jnp.where(at == 1, mid, jnp.where(at == 2, low, 0.0)))
    for d in range(dp):
        tx_ref[d] = coded.astype(BF16)


def passage_kernel(dp, rx2_ref, rx_ref, v_ref, eb_ref, expo_ref, sa_ref, sb_ref, tx_ref, dv_ref, mixed, dv):
    held = 8
    part = rx_ref[0].astype(F32)
    for s in range(1, dp):
        part = part + rx_ref[s].astype(F32)
    sums = query_sums(part)
    inv = 1.0 / jnp.where(sums > 0.0, sums, 1.0)
    wide_inv = jnp.concatenate([inv[k : k + 1] for k in range(dp)], axis=1)
    share = sa_ref[...] * wide_inv - sb_ref[...]
    for p in range(held):
        cut = slice(PROWS * p, PROWS * (p + 1))
        mixed[cut, :] = (expo_ref[cut, :].astype(F32) * share[p : p + 1]).astype(BF16)
    deq = contract(eb_ref[...], mixed[...], ((0,), (0,))).astype(BF16)
    for k in range(dp):
        tx_ref[k] = deq[:, 128 * k : 128 * (k + 1)]
    qt = jnp.concatenate([rx2_ref[k, 0:128, :] for k in range(dp)], axis=1)
    for p in range(held):
        dep = contract(mixed[PROWS * p : PROWS * (p + 1), :], qt, ((1,), (1,)))[0:PLEN]
        v = v_ref[PLEN * p : PLEN * (p + 1), :]
        rp = lax.rsqrt(jnp.sum(v * v, axis=1, keepdims=True) + EPS)
        e = v * rp
        dv[PLEN * p : PLEN * (p + 1), :] = rp * (dep - e * jnp.sum(e * dep, axis=1, keepdims=True))
    dv_ref[...] = dv[...].astype(BF16)


def grad_kernel(dp, hq_ref, hp_ref, w_ref, rx_ref, vt_ref, dvp_ref, gq_ref, gw_ref):
    deq = rx_ref[0].astype(F32)
    for s in range(1, dp):
        deq = deq + rx_ref[s].astype(F32)
    vt = vt_ref[...]
    r = lax.rsqrt(jnp.sum(vt * vt, axis=0, keepdims=True) + EPS)
    et = vt * r
    dvq = (r * (deq - et * jnp.sum(et * deq, axis=0, keepdims=True))).astype(BF16)
    gq_ref[...] = contract(dvq, w_ref[...], ((0,), (1,))).astype(BF16)
    gwt = contract(dvp_ref[...], hp_ref[...], ((0,), (0,)))
    gwt = gwt + jnp.dot(dvq, hq_ref[...], preferred_element_type=F32)
    gw_ref[...] = gwt.T.astype(BF16)


def share_kernel(terms_ref, tx_ref):
    mine = terms_ref[0].astype(F32)
    for m in range(1, terms_ref.shape[0]):
        mine = mine + terms_ref[m].astype(F32)
    for d in range(tx_ref.shape[0]):
        tx_ref[d] = mine


def sum_kernel(shares_ref, out_ref):
    total = shares_ref[0]
    for d in range(1, shares_ref.shape[0]):
        total = total + shares_ref[d]
    out_ref[...] = total


def call(kernel, outs, scratch=(), mib=20, gflop=0):
    return pl.pallas_call(
        kernel,
        out_shape=[jax.ShapeDtypeStruct(s, t) for s, t in outs],
        scratch_shapes=[pltpu.VMEM(*s) if isinstance(s, tuple) else s for s in scratch],
        cost_estimate=pl.CostEstimate(flops=gflop * 10**9, bytes_accessed=4 * 10**6, transcendentals=0),
        compiler_params=pltpu.CompilerParams(vmem_limit_bytes=mib * 1024 * 1024),
    )


def on_device(dp, n_mp, hq, hp, proj_weight, negatives, ranks):
    rows = proj_weight.shape[0]
    width = n_mp * rows
    n_q = dp * 128
    n_p = 8 * PLEN
    (sent,) = call(copies_kernel, [((n_mp,) + proj_weight.shape, BF16)], gflop=8)(proj_weight)
    weight = lax.all_to_all(sent, MP, 0, 0).reshape(width, 128)
    tx2, vt = call(
        functools.partial(query_kernel, dp, n_mp), [((dp, 136, 128), BF16), ((128, 128), F32)], gflop=4
    )(hq, weight, negatives, ranks)
    rx2 = lax.all_to_all(tx2, "dp", 0, 0)
    tx3, v, eb, expo, sa, sb = call(
        functools.partial(score_kernel, dp),
        [
            ((dp, 16, 128), BF16),
            ((n_p, 128), F32),
            ((8 * PROWS, 128), BF16),
            ((8 * PROWS, n_q), BF16),
            ((8, n_q), F32),
            ((8, n_q), F32),
        ],
        [((8 * PROWS, 128), F32), ((16, 128), F32)],
        mib=28,
        gflop=2,
    )(hp, weight, rx2)
    rx3 = lax.all_to_all(tx3, "dp", 0, 0)
    tx4, dvp = call(
        functools.partial(passage_kernel, dp),
        [((dp, 128, 128), BF16), ((n_p, 128), BF16)],
        [((8 * PROWS, n_q), BF16), ((n_p, 128), F32)],
        gflop=1,
    )(rx2, rx3, v, eb, expo, sa, sb)
    rx4 = lax.all_to_all(tx4, "dp", 0, 0)
    grad_queries, gw = call(
        functools.partial(grad_kernel, dp), [((128, width), BF16), ((width, 128), BF16)], gflop=1
    )(hq, hp, weight, rx4, vt, dvp)
    terms = lax.all_to_all(gw.reshape(n_mp, rows, 128), MP, 0, 0)
    (tx5,) = call(share_kernel, [((dp, rows, 128), F32)])(terms)
    shares = lax.all_to_all(tx5, "dp", 0, 0)
    (grad_weight,) = call(sum_kernel, [((rows, 128), F32)])(shares)
    return grad_queries, grad_weight


def solution(mesh):
    dp = mesh.shape["dp"]
    n_mp = mesh.shape["mp"]
    cut = (4, 8, 2) if n_mp == 64 else (n_mp, 1, 1)
    finer = Mesh(mesh.devices.reshape((dp,) + cut), ALL)
    placed = (P(ALL, None), P(ALL, None), P(MP, None), P(ALL, None), P(ALL, None))
    return jax.shard_map(
        functools.partial(on_device, dp, n_mp),
        mesh=finer,
        in_specs=placed,
        out_specs=(P(ALL, None), P(MP, None)),
        check_vma=False,
    )
```

```python
import functools

import jax
import jax.numpy as jnp
from jax import lax
from jax.experimental import pallas as pl
from jax.experimental.pallas import tpu as pltpu
from jax.sharding import Mesh
from jax.sharding import PartitionSpec as P

QLEN = 32
PLEN = 180
PROWS = 192
TAU = 0.1
RANK_TEMP = 8.0
EPS = 1e-06
LOG2E = 1.4426950408889634
F32 = jnp.float32
BF16 = jnp.bfloat16
MP = ("x", "y", "core")
ALL = ("dp", "x", "y", "core")


def contract(a, b, dims):
    return lax.dot_general(a, b, (dims, ((), ())), preferred_element_type=F32)


def lanes(shape):
    return lax.broadcasted_iota(jnp.int32, shape, 1)


def query_sums(x):
    width = x.shape[1]
    for s in (1, 2, 4, 8, 16):
        x = x + pltpu.roll(x, s, 1)
    x = jnp.where(lanes(x.shape) % QLEN == QLEN - 1, x, 0.0)
    for s in (1, 2, 4, 8, 16):
        x = x + pltpu.roll(x, width - s, 1)
    return x


def copies_kernel(w_ref, out_ref):
    for i in range(out_ref.shape[0]):
        out_ref[i] = w_ref[...]


def query_kernel(dp, n_mp, hq_ref, w_ref, neg_ref, rank_ref, tx_ref, vt_ref):
    held = 8
    neg = neg_ref[...]
    place = lax.div(neg, held * n_mp) * held + lax.rem(neg, held)
    teach = jnp.exp(-rank_ref[...].astype(F32) / RANK_TEMP)
    teach = teach / jnp.sum(teach, axis=1, keepdims=True)
    slots = dp * held
    row = lax.broadcasted_iota(jnp.int32, (slots, neg.shape[1]), 0)
    lane = lanes((slots, 128))
    table = jnp.zeros((slots, 128), F32)
    for q in range(neg.shape[0]):
        mine = jnp.where(place[q : q + 1, :] == row, teach[q : q + 1, :], 0.0)
        column = jnp.sum(mine, axis=1, keepdims=True)
        table = jnp.where(lane // QLEN == q, column, table)
    high = table.astype(BF16).astype(F32)
    halves = jnp.where(lane % QLEN < QLEN // 2, high, table - high)
    for d in range(dp):
        tx_ref[d, 128:136, :] = halves[held * d : held * d + held].astype(BF16)
    vt = jnp.dot(hq_ref[...], w_ref[...], preferred_element_type=F32).T
    vt_ref[...] = vt
    et = vt * lax.rsqrt(jnp.sum(vt * vt, axis=0, keepdims=True) + EPS)
    etb = et.astype(BF16)
    for d in range(dp):
        tx_ref[d, 0:128, :] = etb


def score_kernel(dp, hp_ref, w_ref, rx_ref, tx_ref, v_ref, eb_ref, expo_ref, sa_ref, sb_ref, ef, sums):
    held = 8
    v_ref[...] = jnp.dot(hp_ref[...], w_ref[...], preferred_element_type=F32)
    for p in range(held):
        v = v_ref[PLEN * p : PLEN * (p + 1), :]
        ef[PROWS * (p + 1) - 16 : PROWS * (p + 1), :] = jnp.zeros((16, 128), F32)
        ef[PROWS * p : PROWS * p + PLEN, :] = v * lax.rsqrt(jnp.sum(v * v, axis=1, keepdims=True) + EPS)
    eb_ref[...] = ef[...].astype(BF16)
    q = jnp.concatenate([rx_ref[k, 0:128, :] for k in range(dp)], axis=1)
    codes = jnp.concatenate([rx_ref[k, 128:136, :].astype(F32) for k in range(dp)], axis=1)
    half = QLEN // 2
    other = jnp.where(
        lanes(codes.shape) % QLEN < half, pltpu.roll(codes, 128 * dp - half, 1), pltpu.roll(codes, half, 1)
    )
    teach = codes + other
    dots = jnp.dot(eb_ref[...], q, preferred_element_type=F32)
    row = lax.broadcasted_iota(jnp.int32, (8, 128 * dp), 0)
    total = jnp.zeros((8, 128 * dp), F32)
    for p in range(held):
        cut = slice(PROWS * p, PROWS * (p + 1))
        expo = jnp.exp2(dots[cut] * (LOG2E / TAU))
        expo_ref[cut, :] = expo.astype(BF16)
        part = jnp.where(row < PLEN - 176, expo[176:184], 0.0)
        for i in range(22):
            part = part + expo[8 * i : 8 * (i + 1)]
        total = jnp.where(row == p, jnp.sum(part, axis=0, keepdims=True), total)
    score = query_sums(TAU * jnp.log(total))
    es = jnp.where(teach > 0.0, jnp.exp(score), 0.0)
    sa_ref[...] = es / total
    sb_ref[...] = teach / total
    listed = jnp.sum(es, axis=0, keepdims=True)
    sums[...] = jnp.zeros((16, 128), F32)
    for k in range(dp):
        sums[k : k + 1, :] = listed[:, 128 * k : 128 * (k + 1)]
    whole = sums[...]
    high = whole.astype(BF16).astype(F32)
    rest = whole - high
    mid = rest.astype(BF16).astype(F32)
    low = rest - mid
    at = lanes((16, 128)) % QLEN
    coded = jnp.where(at == 0, high, jnp.where(at == 1, mid, jnp.where(at == 2, low, 0.0)))
    packed = (coded[0:8] + pltpu.roll(coded[8:16], QLEN // 2, 1)).astype(BF16)
    for d in range(dp):
        tx_ref[d] = packed


def passage_kernel(dp, rx2_ref, rx_ref, v_ref, eb_ref, expo_ref, sa_ref, sb_ref, tx_ref, dv_ref, mixed, dv):
    held = 8
    part = rx_ref[0].astype(F32)
    for s in range(1, dp):
        part = part + rx_ref[s].astype(F32)
    first = lanes(part.shape) % QLEN < QLEN // 2
    sums = query_sums(jnp.concatenate([jnp.where(first, part, 0.0), jnp.where(first, 0.0, part)], axis=0))
    inv = 1.0 / jnp.where(sums > 0.0, sums, 1.0)
    wide_inv = jnp.concatenate([inv[k : k + 1] for k in range(dp)], axis=1)
    share = sa_ref[...] * wide_inv - sb_ref[...]
    for p in range(held):
        cut = slice(PROWS * p, PROWS * (p + 1))
        mixed[cut, :] = (expo_ref[cut, :].astype(F32) * share[p : p + 1]).astype(BF16)
    deq = contract(eb_ref[...], mixed[...], ((0,), (0,))).astype(BF16)
    for k in range(dp):
        tx_ref[k] = deq[:, 128 * k : 128 * (k + 1)]
    qt = jnp.concatenate([rx2_ref[k, 0:128, :] for k in range(dp)], axis=1)
    for p in range(held):
        dep = contract(mixed[PROWS * p : PROWS * (p + 1), :], qt, ((1,), (1,)))[0:PLEN]
        v = v_ref[PLEN * p : PLEN * (p + 1), :]
        rp = lax.rsqrt(jnp.sum(v * v, axis=1, keepdims=True) + EPS)
        e = v * rp
        dv[PLEN * p : PLEN * (p + 1), :] = rp * (dep - e * jnp.sum(e * dep, axis=1, keepdims=True))
    dv_ref[...] = dv[...].astype(BF16)


def grad_kernel(dp, hq_ref, hp_ref, w_ref, rx_ref, vt_ref, dvp_ref, gq_ref, gw_ref):
    deq = rx_ref[0].astype(F32)
    for s in range(1, dp):
        deq = deq + rx_ref[s].astype(F32)
    vt = vt_ref[...]
    r = lax.rsqrt(jnp.sum(vt * vt, axis=0, keepdims=True) + EPS)
    et = vt * r
    dvq = (r * (deq - et * jnp.sum(et * deq, axis=0, keepdims=True))).astype(BF16)
    gq_ref[...] = contract(dvq, w_ref[...], ((0,), (1,))).astype(BF16)
    gwt = contract(dvp_ref[...], hp_ref[...], ((0,), (0,)))
    gwt = gwt + jnp.dot(dvq, hq_ref[...], preferred_element_type=F32)
    gw_ref[...] = gwt.T.astype(BF16)


def share_kernel(terms_ref, tx_ref):
    mine = terms_ref[0].astype(F32)
    for m in range(1, terms_ref.shape[0]):
        mine = mine + terms_ref[m].astype(F32)
    sent = mine.astype(BF16)
    for d in range(tx_ref.shape[0]):
        tx_ref[d] = sent


def sum_kernel(shares_ref, out_ref):
    total = shares_ref[0].astype(F32)
    for d in range(1, shares_ref.shape[0]):
        total = total + shares_ref[d].astype(F32)
    out_ref[...] = total


def call(kernel, outs, scratch=(), mib=20, gflop=0):
    return pl.pallas_call(
        kernel,
        out_shape=[jax.ShapeDtypeStruct(s, t) for s, t in outs],
        scratch_shapes=[pltpu.VMEM(*s) if isinstance(s, tuple) else s for s in scratch],
        cost_estimate=pl.CostEstimate(flops=gflop * 10**9, bytes_accessed=4 * 10**6, transcendentals=0),
        compiler_params=pltpu.CompilerParams(vmem_limit_bytes=mib * 1024 * 1024),
    )


def on_device(dp, n_mp, hq, hp, proj_weight, negatives, ranks):
    rows = proj_weight.shape[0]
    width = n_mp * rows
    n_q = dp * 128
    n_p = 8 * PLEN
    (sent,) = call(copies_kernel, [((n_mp,) + proj_weight.shape, BF16)], gflop=8)(proj_weight)
    weight = lax.all_to_all(sent, MP, 0, 0).reshape(width, 128)
    tx2, vt = call(
        functools.partial(query_kernel, dp, n_mp), [((dp, 136, 128), BF16), ((128, 128), F32)], gflop=4
    )(hq, weight, negatives, ranks)
    rx2 = lax.all_to_all(tx2, "dp", 0, 0)
    tx3, v, eb, expo, sa, sb = call(
        functools.partial(score_kernel, dp),
        [
            ((dp, 8, 128), BF16),
            ((n_p, 128), F32),
            ((8 * PROWS, 128), BF16),
            ((8 * PROWS, n_q), BF16),
            ((8, n_q), F32),
            ((8, n_q), F32),
        ],
        [((8 * PROWS, 128), F32), ((16, 128), F32)],
        mib=28,
        gflop=2,
    )(hp, weight, rx2)
    rx3 = lax.all_to_all(tx3, "dp", 0, 0)
    tx4, dvp = call(
        functools.partial(passage_kernel, dp),
        [((dp, 128, 128), BF16), ((n_p, 128), BF16)],
        [((8 * PROWS, n_q), BF16), ((n_p, 128), F32)],
        gflop=1,
    )(rx2, rx3, v, eb, expo, sa, sb)
    rx4 = lax.all_to_all(tx4, "dp", 0, 0)
    grad_queries, gw = call(
        functools.partial(grad_kernel, dp), [((128, width), BF16), ((width, 128), BF16)], gflop=1
    )(hq, hp, weight, rx4, vt, dvp)
    terms = lax.all_to_all(gw.reshape(n_mp, rows, 128), MP, 0, 0)
    (tx5,) = call(share_kernel, [((dp, rows, 128), BF16)])(terms)
    shares = lax.all_to_all(tx5, "dp", 0, 0)
    (grad_weight,) = call(sum_kernel, [((rows, 128), F32)])(shares)
    return grad_queries, grad_weight


def solution(mesh):
    dp = mesh.shape["dp"]
    n_mp = mesh.shape["mp"]
    cut = (4, 8, 2) if n_mp == 64 else (n_mp, 1, 1)
    finer = Mesh(mesh.devices.reshape((dp,) + cut), ALL)
    placed = (P(ALL, None), P(ALL, None), P(MP, None), P(ALL, None), P(ALL, None))
    return jax.shard_map(
        functools.partial(on_device, dp, n_mp),
        mesh=finer,
        in_specs=placed,
        out_specs=(P(ALL, None), P(MP, None)),
        check_vma=False,
    )
```

```python
import functools

import jax
import jax.numpy as jnp
from jax import lax
from jax.experimental import pallas as pl
from jax.experimental.pallas import tpu as pltpu
from jax.sharding import Mesh
from jax.sharding import PartitionSpec as P

QLEN = 32
PLEN = 180
PROWS = 192
TAU = 0.1
RANK_TEMP = 8.0
EPS = 1e-06
LOG2E = 1.4426950408889634
F32 = jnp.float32
BF16 = jnp.bfloat16
MP = ("x", "y", "core")
ALL = ("dp", "x", "y", "core")


def contract(a, b, dims):
    return lax.dot_general(a, b, (dims, ((), ())), preferred_element_type=F32)


def lanes(shape):
    return lax.broadcasted_iota(jnp.int32, shape, 1)


def query_sums(x):
    width = x.shape[1]
    for s in (1, 2, 4, 8, 16):
        x = x + pltpu.roll(x, s, 1)
    x = jnp.where(lanes(x.shape) % QLEN == QLEN - 1, x, 0.0)
    for s in (1, 2, 4, 8, 16):
        x = x + pltpu.roll(x, width - s, 1)
    return x


def copies_kernel(w_ref, out_ref):
    for i in range(out_ref.shape[0]):
        out_ref[i] = w_ref[...]


def query_kernel(dp, n_mp, hq_ref, w_ref, neg_ref, rank_ref, tx_ref, vt_ref):
    held = 8
    neg = neg_ref[...]
    place = lax.div(neg, held * n_mp) * held + lax.rem(neg, held)
    teach = jnp.exp(-rank_ref[...].astype(F32) / RANK_TEMP)
    teach = teach / jnp.sum(teach, axis=1, keepdims=True)
    slots = dp * held
    row = lax.broadcasted_iota(jnp.int32, (slots, neg.shape[1]), 0)
    lane = lanes((slots, 128))
    table = jnp.zeros((slots, 128), F32)
    for q in range(neg.shape[0]):
        mine = jnp.where(place[q : q + 1, :] == row, teach[q : q + 1, :], 0.0)
        column = jnp.sum(mine, axis=1, keepdims=True)
        table = jnp.where(lane // QLEN == q, column, table)
    high = table.astype(BF16).astype(F32)
    halves = jnp.where(lane % QLEN < QLEN // 2, high, table - high)
    for d in range(dp):
        tx_ref[d, 128:136, :] = halves[held * d : held * d + held].astype(BF16)
    vt = jnp.dot(hq_ref[...], w_ref[...], preferred_element_type=F32).T
    vt_ref[...] = vt
    et = vt * lax.rsqrt(jnp.sum(vt * vt, axis=0, keepdims=True) + EPS)
    etb = et.astype(BF16)
    for d in range(dp):
        tx_ref[d, 0:128, :] = etb


def score_kernel(dp, hp_ref, w_ref, rx_ref, tx_ref, v_ref, eb_ref, expo_ref, sa_ref, sb_ref, ef, sums):
    held = 8
    v_ref[...] = jnp.dot(hp_ref[...], w_ref[...], preferred_element_type=F32)
    for p in range(held):
        v = v_ref[PLEN * p : PLEN * (p + 1), :]
        ef[PROWS * (p + 1) - 16 : PROWS * (p + 1), :] = jnp.zeros((16, 128), F32)
        ef[PROWS * p : PROWS * p + PLEN, :] = v * lax.rsqrt(jnp.sum(v * v, axis=1, keepdims=True) + EPS)
    eb_ref[...] = ef[...].astype(BF16)
    q = jnp.concatenate([rx_ref[k, 0:128, :] for k in range(dp)], axis=1)
    codes = jnp.concatenate([rx_ref[k, 128:136, :].astype(F32) for k in range(dp)], axis=1)
    half = QLEN // 2
    other = jnp.where(
        lanes(codes.shape) % QLEN < half, pltpu.roll(codes, 128 * dp - half, 1), pltpu.roll(codes, half, 1)
    )
    teach = codes + other
    dots = jnp.dot(eb_ref[...], q, preferred_element_type=F32)
    row = lax.broadcasted_iota(jnp.int32, (8, 128 * dp), 0)
    total = jnp.zeros((8, 128 * dp), F32)
    for p in range(held):
        cut = slice(PROWS * p, PROWS * (p + 1))
        expo = jnp.exp2(dots[cut] * (LOG2E / TAU))
        expo_ref[cut, :] = expo.astype(BF16)
        part = jnp.where(row < PLEN - 176, expo[176:184], 0.0)
        for i in range(22):
            part = part + expo[8 * i : 8 * (i + 1)]
        total = jnp.where(row == p, jnp.sum(part, axis=0, keepdims=True), total)
    score = query_sums(TAU * jnp.log(total))
    es = jnp.where(teach > 0.0, jnp.exp(score), 0.0)
    sa_ref[...] = es / total
    sb_ref[...] = teach / total
    listed = jnp.sum(es, axis=0, keepdims=True)
    sums[...] = jnp.zeros((16, 128), F32)
    for k in range(dp):
        sums[k : k + 1, :] = listed[:, 128 * k : 128 * (k + 1)]
    whole = sums[...]
    high = whole.astype(BF16).astype(F32)
    rest = whole - high
    mid = rest.astype(BF16).astype(F32)
    low = rest - mid
    at = lanes((16, 128)) % QLEN
    coded = jnp.where(at == 0, high, jnp.where(at == 1, mid, jnp.where(at == 2, low, 0.0)))
    packed = (coded[0:8] + pltpu.roll(coded[8:16], QLEN // 2, 1)).astype(BF16)
    for d in range(dp):
        tx_ref[d] = packed


def passage_kernel(dp, rx2_ref, rx_ref, v_ref, eb_ref, expo_ref, sa_ref, sb_ref, tx_ref, dv_ref, mixed, dv):
    held = 8
    part = rx_ref[0].astype(F32)
    for s in range(1, dp):
        part = part + rx_ref[s].astype(F32)
    first = lanes(part.shape) % QLEN < QLEN // 2
    sums = query_sums(jnp.concatenate([jnp.where(first, part, 0.0), jnp.where(first, 0.0, part)], axis=0))
    inv = 1.0 / jnp.where(sums > 0.0, sums, 1.0)
    wide_inv = jnp.concatenate([inv[k : k + 1] for k in range(dp)], axis=1)
    share = sa_ref[...] * wide_inv - sb_ref[...]
    for p in range(held):
        cut = slice(PROWS * p, PROWS * (p + 1))
        mixed[cut, :] = (expo_ref[cut, :].astype(F32) * share[p : p + 1]).astype(BF16)
    deq = contract(eb_ref[...], mixed[...], ((0,), (0,))).astype(BF16)
    for k in range(dp):
        tx_ref[k] = deq[:, 128 * k : 128 * (k + 1)]
    qt = jnp.concatenate([rx2_ref[k, 0:128, :] for k in range(dp)], axis=1)
    for p in range(held):
        dep = contract(mixed[PROWS * p : PROWS * (p + 1), :], qt, ((1,), (1,)))[0:PLEN]
        v = v_ref[PLEN * p : PLEN * (p + 1), :]
        rp = lax.rsqrt(jnp.sum(v * v, axis=1, keepdims=True) + EPS)
        e = v * rp
        dv[PLEN * p : PLEN * (p + 1), :] = rp * (dep - e * jnp.sum(e * dep, axis=1, keepdims=True))
    dv_ref[...] = dv[...].astype(BF16)


def grad_kernel(dp, hq_ref, hp_ref, rx_ref, vt_ref, dvp_ref, dvq_ref, gw_ref):
    deq = rx_ref[0].astype(F32)
    for s in range(1, dp):
        deq = deq + rx_ref[s].astype(F32)
    vt = vt_ref[...]
    r = lax.rsqrt(jnp.sum(vt * vt, axis=0, keepdims=True) + EPS)
    et = vt * r
    dvq = (r * (deq - et * jnp.sum(et * deq, axis=0, keepdims=True))).astype(BF16)
    dvq_ref[...] = dvq
    gwt = contract(dvp_ref[...], hp_ref[...], ((0,), (0,)))
    gwt = gwt + jnp.dot(dvq, hq_ref[...], preferred_element_type=F32)
    gw_ref[...] = gwt.T.astype(BF16)


def share_kernel(terms_ref, tx_ref):
    mine = terms_ref[0].astype(F32)
    for m in range(1, terms_ref.shape[0]):
        mine = mine + terms_ref[m].astype(F32)
    sent = mine.astype(BF16)
    for d in range(tx_ref.shape[0]):
        tx_ref[d] = sent


def last_kernel(shares_ref, dvq_ref, w_ref, gq_ref, out_ref):
    gq_ref[...] = contract(dvq_ref[...], w_ref[...], ((0,), (1,))).astype(BF16)
    total = shares_ref[0].astype(F32)
    for d in range(1, shares_ref.shape[0]):
        total = total + shares_ref[d].astype(F32)
    out_ref[...] = total


def call(kernel, outs, scratch=(), mib=20, gflop=0):
    return pl.pallas_call(
        kernel,
        out_shape=[jax.ShapeDtypeStruct(s, t) for s, t in outs],
        scratch_shapes=[pltpu.VMEM(*s) if isinstance(s, tuple) else s for s in scratch],
        cost_estimate=pl.CostEstimate(flops=gflop * 10**9, bytes_accessed=4 * 10**6, transcendentals=0),
        compiler_params=pltpu.CompilerParams(vmem_limit_bytes=mib * 1024 * 1024),
    )


def on_device(dp, n_mp, hq, hp, proj_weight, negatives, ranks):
    rows = proj_weight.shape[0]
    width = n_mp * rows
    n_q = dp * 128
    n_p = 8 * PLEN
    (sent,) = call(copies_kernel, [((n_mp,) + proj_weight.shape, BF16)], gflop=8)(proj_weight)
    weight = lax.all_to_all(sent, MP, 0, 0).reshape(width, 128)
    tx2, vt = call(
        functools.partial(query_kernel, dp, n_mp), [((dp, 136, 128), BF16), ((128, 128), F32)], gflop=4
    )(hq, weight, negatives, ranks)
    rx2 = lax.all_to_all(tx2, "dp", 0, 0)
    tx3, v, eb, expo, sa, sb = call(
        functools.partial(score_kernel, dp),
        [
            ((dp, 8, 128), BF16),
            ((n_p, 128), F32),
            ((8 * PROWS, 128), BF16),
            ((8 * PROWS, n_q), BF16),
            ((8, n_q), F32),
            ((8, n_q), F32),
        ],
        [((8 * PROWS, 128), F32), ((16, 128), F32)],
        mib=28,
        gflop=2,
    )(hp, weight, rx2)
    rx3 = lax.all_to_all(tx3, "dp", 0, 0)
    tx4, dvp = call(
        functools.partial(passage_kernel, dp),
        [((dp, 128, 128), BF16), ((n_p, 128), BF16)],
        [((8 * PROWS, n_q), BF16), ((n_p, 128), F32)],
        gflop=1,
    )(rx2, rx3, v, eb, expo, sa, sb)
    rx4 = lax.all_to_all(tx4, "dp", 0, 0)
    dvq, gw = call(
        functools.partial(grad_kernel, dp), [((128, 128), BF16), ((width, 128), BF16)], gflop=1
    )(hq, hp, rx4, vt, dvp)
    terms = lax.all_to_all(gw.reshape(n_mp, rows, 128), MP, 0, 0)
    (tx5,) = call(share_kernel, [((dp, rows, 128), BF16)])(terms)
    shares = lax.all_to_all(tx5, "dp", 0, 0)
    grad_queries, grad_weight = call(last_kernel, [((128, width), BF16), ((rows, 128), F32)])(shares, dvq, weight)
    return grad_queries, grad_weight


def solution(mesh):
    dp = mesh.shape["dp"]
    n_mp = mesh.shape["mp"]
    cut = (4, 8, 2) if n_mp == 64 else (n_mp, 1, 1)
    finer = Mesh(mesh.devices.reshape((dp,) + cut), ALL)
    placed = (P(ALL, None), P(ALL, None), P(MP, None), P(ALL, None), P(ALL, None))
    return jax.shard_map(
        functools.partial(on_device, dp, n_mp),
        mesh=finer,
        in_specs=placed,
        out_specs=(P(ALL, None), P(MP, None)),
        check_vma=False,
    )
```
